32 devices in a mesh: section: 4 (over y, x), tensor: 2 (over core), dp: 4 (over z).
Axes of the slice: x: 2, y: 2, z: 4, core: 2. Of those that a mesh axis runs over, the one named last changes fastest.
Arguments:
- hidden: bfloat16 [4, 64, 8192], P('dp'), may hold values from -6 to 6
- lengths: int32 [4, 4], replicated, may hold values from 1 to 48, 64 in all within a row
- targets: int32 [4, 64], replicated, may hold values from 0 to 65535
- attn_gain: float32 [4, 8192], P('section'), may hold values from 0.25 to 1.75
- w_query: bfloat16 [4, 8192, 4096], P('section', None, ('tensor', 'dp')), as said below
- w_key: bfloat16 [4, 8192, 512], P('section', None, 'tensor'), may hold values from -0.0625 to 0.0625
- w_value: bfloat16 [4, 8192, 512], P('section', None, 'tensor'), may hold values from -0.0625 to 0.0625
- w_out: bfloat16 [4, 4096, 8192], P('section', ('tensor', 'dp')), may hold values from -0.09375 to 0.09375
- final_gain: float32 [8192], replicated, may hold values from 0.25 to 1.75
- unembed: bfloat16 [8192, 65536], P(None, ('section', 'tensor', 'dp')), as said below
Outputs:
- logprob: float32 [4, 64], replicated
The draws below stay inside these ranges and needn't reach their ends.
Inputs may be any that keep to these rules, and one draw needn't show every extreme that they name: Each row's 4 lengths sum to 64; in every row the longest is exactly 48. `w_query`: real-valued projection weights. `unembed`: real-valued output embedding.
All inputs are finite; a program needn't handle non-finite values.
Results may differ from the reference program's by a relative error of at most 0.018.
The reference program's roundings to bfloat16 on the way count: a program that leaves them out, or rounds other values in their place, can miss the bound.
Values may be sent and summed in bfloat16 or wider, within the bound.
A program may use at most 256 MiB of HBM per device.

```python
import math
import jax
import jax.numpy as jnp
import numpy as np
from jax import lax

D = 8192
HEADS = 64
HD = 64
KVH = 8
VOCAB = 65536
S = 64
SEQS = 4
MOST = 48
LAYERS = 4
ROWS = 4


def draw_w_query(key, part):
    key = jax.random.fold_in(key, 11)
    values = jax.random.normal(key, (LAYERS, D, HEADS * HD), jnp.float32) * D ** (-0.5)
    return values.astype(jnp.bfloat16)


def draw_unembed(key, part):
    key = jax.random.fold_in(key, 23)
    values = jax.random.normal(key, (D, VOCAB), jnp.float32) * (3.0 * D ** (-0.5))
    return values.astype(jnp.bfloat16)


def plant(drawn, own_key, low, top_value):
    spot = [jax.random.randint(jax.random.fold_in(own_key, axis), (), 0, length) for axis, length in enumerate(drawn.shape)]
    widest = drawn.shape.index(max(drawn.shape))
    beside = spot[:widest] + [(spot[widest] + 1) % drawn.shape[widest]] + spot[widest + 1:]
    return drawn.at[tuple(spot)].set(low).at[tuple(beside)].set(top_value)


def levels(own_key, shape, cuts, smallest, largest):
    loudness, own = 1.0, jax.random.fold_in(own_key, 6)
    for axis_at, parts in cuts:
        heights = jnp.exp(jax.random.uniform(jax.random.fold_in(own, axis_at), (parts,), jnp.float32, smallest / len(cuts), largest / len(cuts)))
        loudness = loudness * jnp.repeat(heights, shape[axis_at] // parts).reshape([-1 if axis == axis_at else 1 for axis in range(len(shape))])
    return loudness


def rank_bounds(count, lean):
    loads = [(1 << 20) // math.isqrt(rank ** lean) + 1 for rank in range(1, count + 1)]
    scale = 1 + sum(loads) // (1 << 30)
    return np.cumsum(np.array([max(1, weight // scale) for weight in loads]))


def skewed_ids(own_key, shape, number_of, slope):
    grid = rank_bounds(number_of, slope)
    ticket = jax.random.randint(jax.random.fold_in(own_key, 1), shape, 0, int(grid[number_of - 1]))
    standing = jnp.searchsorted(jnp.asarray(grid, jnp.int32), ticket, side="right")
    return jax.random.permutation(jax.random.fold_in(own_key, 2), number_of)[standing].astype(jnp.int32)


def profile(number_of, total, bound, slope):
    loads = [(1 << 20) // math.isqrt(standing ** slope) + 1 for standing in range(2, number_of + 1)]
    spare, counts = total - bound - (number_of - 1), [1] * (number_of - 1)
    while spare > 0:
        free = [i for i in range(number_of - 1) if counts[i] < bound]
        mass, budget = sum([loads[i] for i in free]), spare
        for i in free:
            extra = min(bound - counts[i], max(1, budget * loads[i] // mass), spare)
            counts[i] = counts[i] + extra
            spare = spare - extra
    return np.array([bound] + counts)


def uneven(key, amount, total, most, lean):
    if amount == 2:
        one = jax.random.randint(key, (), max(1, total - most), min(most, total - 1) + 1)
        return jnp.stack([one, total - one])
    sizes = jnp.asarray(profile(amount, total, most, lean), jnp.int32)
    pairs = (amount - 1) // 2
    giver, receiver = sizes[1:1 + 2 * pairs:2], sizes[2:2 + 2 * pairs:2]
    room = jnp.minimum(giver - 1, most - receiver)
    moved = jax.random.randint(jax.random.fold_in(key, 1), (pairs,), 0, 1 << 20) % (room + 1)
    sizes = sizes.at[1:1 + 2 * pairs:2].set(giver - moved).at[2:2 + 2 * pairs:2].set(receiver + moved)
    return sizes[jax.random.permutation(jax.random.fold_in(key, 2), amount)]


def gaussian(key, extent, width, limit, cuts=(), kind=jnp.bfloat16):
    array = width * jax.random.normal(key, extent, jnp.float32)
    if cuts:
        array = array * levels(key, extent, cuts, -0.22, 0.18)
    return jnp.clip(array, -limit, limit).astype(kind)


def setup_inputs(seed: int = 0) -> dict:
    key_list = jax.random.split(jax.random.key(seed), 11)
    return {
        "hidden": gaussian(key_list[0], (ROWS, S, D), 1.0, 6.0, ((0, 4),)),
        "lengths": jax.vmap(lambda own: uneven(own, SEQS, S, MOST, 2))(jax.random.split(key_list[1], ROWS)).reshape((ROWS, SEQS)).astype(jnp.int32),
        "targets": plant(skewed_ids(key_list[2], (ROWS, S), VOCAB, 2), jax.random.fold_in(key_list[2], 3), 0, VOCAB - 1).astype(jnp.int32),
        "attn_gain": jnp.clip(1.0 + 0.15 * jax.random.normal(key_list[3], (LAYERS, D), jnp.float32), 0.25, 1.75),
        "w_query": draw_w_query(jax.random.fold_in(key_list[10], 71), 0),
        "w_key": gaussian(key_list[5], (LAYERS, D, KVH * HD), D ** -0.5, 0.0625, ((0, 4), (2, 2))),
        "w_value": gaussian(key_list[6], (LAYERS, D, KVH * HD), D ** -0.5, 0.0625, ((0, 4), (2, 2))),
        "w_out": gaussian(key_list[7], (LAYERS, HEADS * HD, D), (HEADS * HD) ** -0.5, 0.09375, ((0, 4), (1, 8))),
        "final_gain": jnp.clip(1.0 + 0.15 * jax.random.normal(key_list[8], (D,), jnp.float32), 0.25, 1.75),
        "unembed": draw_unembed(jax.random.fold_in(key_list[10], 71), 0),
    }


EPS = 1e-05
ROPE_BASE = 500000.0
NEGATIVE = -1e+30

def norm_round(block_rows, gain_row):
    widened = block_rows.astype(jnp.float32)
    inverse = lax.rsqrt(lax.optimization_barrier(jnp.mean(widened * widened, axis=-1, keepdims=True)) + EPS)
    return (widened * inverse * gain_row).astype(jnp.bfloat16)

def segments(lengths, length):
    seq_ends = jnp.cumsum(lengths, axis=-1, dtype=jnp.int32)
    places = jnp.arange(length, dtype=jnp.int32)
    passed = seq_ends[:, None, :] <= places[None, :, None]
    owners = lax.optimization_barrier(jnp.sum(passed.astype(jnp.int32), axis=-1, dtype=jnp.int32))
    offset = lax.optimization_barrier(jnp.sum(jnp.where(passed, lengths[:, None, :], 0), axis=-1, dtype=jnp.int32))
    return (owners, places[None, :] - offset)

def rotate(values, positions):
    half_dim = values.shape[-1] // 2
    frequency = jnp.power(ROPE_BASE, -2.0 * jnp.arange(half_dim, dtype=jnp.float32) / values.shape[-1])
    angles = positions.astype(jnp.float32)[..., None] * frequency
    cosines = jnp.cos(angles)[..., None, :]
    sine_vals = jnp.sin(angles)[..., None, :]
    front_half = values[..., :half_dim]
    back_half = values[..., half_dim:]
    return jnp.concatenate([front_half * cosines - back_half * sine_vals, back_half * cosines + front_half * sine_vals], axis=-1)

def attend(queries, key_rows, value_rows, key_head, key_owner, query_owner, query_place):
    picked_keys = jnp.take(key_rows, key_head, axis=2).astype(jnp.float32)
    picked_values = jnp.take(value_rows, key_head, axis=2).astype(jnp.float32)
    scores = jnp.einsum('gphd,gshd->ghps', queries.astype(jnp.float32), picked_keys) * queries.shape[-1] ** (-0.5)
    key_place = jnp.arange(key_rows.shape[1], dtype=jnp.int32)
    allowed = (key_owner[:, None, :] == query_owner[:, :, None]) & (key_place[None, None, :] <= query_place[None, :, None])
    allowed = allowed[:, None, :, :]
    highest = lax.optimization_barrier(jnp.max(jnp.where(allowed, scores, NEGATIVE), axis=-1, keepdims=True))
    raised = jnp.where(allowed, jnp.exp(scores - highest), 0.0)
    weights = (raised / lax.optimization_barrier(jnp.sum(raised, axis=-1, keepdims=True))).astype(jnp.bfloat16)
    mixture = jnp.einsum('ghps,gshd->gphd', weights.astype(jnp.float32), picked_values)
    return mixture.astype(jnp.bfloat16)

def reference(hidden, lengths, targets, attn_gain, w_query, w_key, w_value, w_out, final_gain, unembed):
    row_count = hidden.shape[0]
    owners, places_all = segments(lengths, S)
    key_head = jnp.arange(HEADS, dtype=jnp.int32) // (HEADS // KVH)
    positions = jnp.arange(S, dtype=jnp.int32)
    carried = hidden
    for layer_at in range(LAYERS):
        normed = norm_round(carried, attn_gain[layer_at])
        widened = normed.astype(jnp.float32)
        queries = jnp.einsum('rsd,dc->rsc', widened, w_query[layer_at].astype(jnp.float32)).reshape(row_count, S, HEADS, HD)
        key_rows = jnp.einsum('rsd,dc->rsc', widened, w_key[layer_at].astype(jnp.float32)).reshape(row_count, S, KVH, HD)
        value_rows = jnp.einsum('rsd,dc->rsc', widened, w_value[layer_at].astype(jnp.float32)).reshape(row_count, S, KVH, HD)
        queries = rotate(queries, places_all).astype(jnp.bfloat16)
        key_rows = rotate(key_rows, places_all).astype(jnp.bfloat16)
        value_rows = value_rows.astype(jnp.bfloat16)
        attended = attend(queries, key_rows, value_rows, key_head, owners, owners, positions)
        summed = jnp.einsum('rsc,cd->rsd', attended.reshape(row_count, S, HEADS * HD).astype(jnp.float32), w_out[layer_at].astype(jnp.float32))
        carried = (carried.astype(jnp.float32) + summed).astype(jnp.bfloat16)
    normed = norm_round(carried, final_gain).reshape(row_count * S, D)
    logits = jnp.dot(normed, unembed, preferred_element_type=jnp.float32)
    highest = lax.optimization_barrier(jnp.max(logits, axis=-1))
    summed_exp = lax.optimization_barrier(jnp.sum(jnp.exp(logits - highest[:, None]), axis=-1))
    chosen = jnp.take_along_axis(logits, targets.reshape(-1, 1).astype(jnp.int32), axis=1)[:, 0]
    return (chosen - highest - jnp.log(summed_exp)).reshape(row_count, S)
```

```python
import jax
import jax.numpy as jnp
from jax import lax
from jax.sharding import PartitionSpec as P

HEADS = 64
HD = 64
KVH = 8


EPS = 1e-05
ROPE_BASE = 500000.0
NEGATIVE = -1e30


def shifted(value, axis, steps):
    count = lax.axis_size(axis)
    pairs = [(source, (source + steps) % count) for source in range(count)]
    return lax.ppermute(value, axis, pairs)


def from_root(x, axis, root):
    mine = lax.axis_index(axis) == root
    return lax.psum(jnp.where(mine, x, jnp.zeros_like(x)), axis)


def norm_round(block_rows, gain_row):
    widened = block_rows.astype(jnp.float32)
    inverse = lax.rsqrt(jnp.mean(widened * widened, axis=-1, keepdims=True) + EPS)
    return (widened * inverse * gain_row).astype(jnp.bfloat16)


def segments(lengths, length):
    seq_ends = jnp.cumsum(lengths, axis=-1, dtype=jnp.int32)
    places = jnp.arange(length, dtype=jnp.int32)
    passed = seq_ends[:, None, :] <= places[None, :, None]
    owners = jnp.sum(passed.astype(jnp.int32), axis=-1, dtype=jnp.int32)
    offset = jnp.sum(jnp.where(passed, lengths[:, None, :], 0), axis=-1, dtype=jnp.int32)
    return (owners, places[None, :] - offset)


def rotate(values, positions):
    half_dim = values.shape[-1] // 2
    frequency = jnp.power(
        ROPE_BASE, -2.0 * jnp.arange(half_dim, dtype=jnp.float32) / values.shape[-1]
    )
    angles = positions.astype(jnp.float32)[..., None] * frequency
    cosines = jnp.cos(angles)[..., None, :]
    sine_vals = jnp.sin(angles)[..., None, :]
    front_half = values[..., :half_dim]
    back_half = values[..., half_dim:]
    return jnp.concatenate(
        [
            front_half * cosines - back_half * sine_vals,
            back_half * cosines + front_half * sine_vals,
        ],
        axis=-1,
    )


def attend(queries, key_rows, value_rows, key_owner, query_owner, query_place):
    scores = jnp.einsum(
        "gphd,gsd->ghps", queries, key_rows, preferred_element_type=jnp.float32
    ) * queries.shape[-1] ** (-0.5)
    key_place = jnp.arange(key_rows.shape[1], dtype=jnp.int32)
    allowed = (key_owner[:, None, :] == query_owner[:, :, None]) & (
        key_place[None, None, :] <= query_place[None, :, None]
    )
    allowed = allowed[:, None, :, :]
    highest = jnp.max(jnp.where(allowed, scores, NEGATIVE), axis=-1, keepdims=True)
    raised = jnp.where(allowed, jnp.exp(scores - highest), 0.0)
    weights = (raised / jnp.sum(raised, axis=-1, keepdims=True)).astype(jnp.bfloat16)
    mixture = jnp.einsum(
        "ghps,gsd->gphd", weights, value_rows, preferred_element_type=jnp.float32
    )
    return mixture.astype(jnp.bfloat16)


def on_device(
    hidden, lengths, targets, attn_gain, w_query, w_key, w_value, w_out, final_gain, unembed
):
    phases = lax.axis_size("section")
    tensor_size = lax.axis_size("tensor")
    groups = lax.axis_size("dp")
    phase_at = lax.axis_index("section")
    tensor_at = lax.axis_index("tensor")
    group_at = lax.axis_index("dp")
    length = hidden.shape[1]
    model_width = hidden.shape[2]
    blocks = 4
    span_rows = length // blocks
    share_rows = span_rows // tensor_size
    gain_row = attn_gain[0]
    query_weight = w_query[0]
    key_weight = w_key[0]
    value_weight = w_value[0]
    out_weight = w_out[0]
    local_heads = query_weight.shape[1] // HD
    owners_all, places_all = segments(lengths, length)
    local_kv = key_weight.shape[1] // HD
    first_head = (tensor_at * groups + group_at) * local_heads
    kv_col = (first_head // (HEADS // KVH) - tensor_at * local_kv) * HD
    kv_weight = jnp.concatenate(
        [
            lax.dynamic_slice_in_dim(key_weight, kv_col, HD, 1),
            lax.dynamic_slice_in_dim(value_weight, kv_col, HD, 1),
        ],
        axis=1,
    )

    def layer(entering, item_at, active, key_cache, value_cache):
        normed = norm_round(entering, gain_row)
        gathered = lax.all_gather(normed, ("dp", "tensor"), axis=0, tiled=True)
        queries = jnp.dot(gathered, query_weight, preferred_element_type=jnp.float32)
        both = jnp.dot(gathered, kv_weight, preferred_element_type=jnp.float32)
        block_start = item_at * span_rows
        block_places = lax.dynamic_slice_in_dim(places_all, block_start, span_rows, 1)
        block_owners = lax.dynamic_slice_in_dim(owners_all, block_start, span_rows, 1)
        queries = rotate(
            queries.reshape(groups, span_rows, local_heads, HD), block_places
        ).astype(jnp.bfloat16)
        key_rows = rotate(both[:, :HD].reshape(groups, span_rows, 1, HD), block_places)
        key_rows = key_rows.reshape(groups, span_rows, HD).astype(jnp.bfloat16)
        value_rows = both[:, HD:].reshape(groups, span_rows, HD).astype(jnp.bfloat16)
        key_cache = jnp.where(
            active, lax.dynamic_update_slice_in_dim(key_cache, key_rows, block_start, 1), key_cache
        )
        value_cache = jnp.where(
            active,
            lax.dynamic_update_slice_in_dim(value_cache, value_rows, block_start, 1),
            value_cache,
        )
        query_place = block_start + jnp.arange(span_rows, dtype=jnp.int32)
        attended = attend(
            queries, key_cache, value_cache, owners_all, block_owners, query_place
        )
        flattened = attended.reshape(groups * span_rows, local_heads * HD)
        summed = lax.psum_scatter(
            jnp.dot(flattened, out_weight, preferred_element_type=jnp.float32),
            ("dp", "tensor"),
            scatter_dimension=0,
            tiled=True,
        )
        updated = (entering.astype(jnp.float32) + summed).astype(jnp.bfloat16)
        return (updated, key_cache, value_cache)

    def entry_rows(step_at):
        item_at = jnp.clip(step_at, 0, blocks - 1)
        return lax.dynamic_slice_in_dim(
            hidden[0], item_at * span_rows + tensor_at * share_rows, share_rows, 0
        )

    def store_final(finished, current, step_at):
        slot_at = step_at - phases
        storing = (phase_at == 0) & (slot_at >= 0) & (slot_at < blocks)
        placed = lax.dynamic_update_slice_in_dim(
            finished, current[None], jnp.clip(slot_at, 0, blocks - 1), 0
        )
        return jnp.where(storing, placed, finished)

    def advance(step_at, carried):
        current, key_cache, value_cache, finished = carried
        finished = store_final(finished, current, step_at)
        item_at = step_at - phase_at
        active = (item_at >= 0) & (item_at < blocks)
        entering = jnp.where(phase_at == 0, entry_rows(step_at), current)
        updated, key_cache, value_cache = layer(
            entering, jnp.clip(item_at, 0, blocks - 1), active, key_cache, value_cache
        )
        current = shifted(updated, "section", 1)
        return (current, key_cache, value_cache, finished)

    cache_shape = (groups, length, HD)
    initial = (
        jnp.zeros((share_rows, model_width), jnp.bfloat16),
        jnp.zeros(cache_shape, jnp.bfloat16),
        jnp.zeros(cache_shape, jnp.bfloat16),
        jnp.zeros((blocks, share_rows, model_width), jnp.bfloat16),
    )
    carried = lax.fori_loop(0, blocks + phases - 1, advance, initial)
    finished = store_final(carried[3], carried[0], blocks + phases - 1)
    normed_final = norm_round(finished.reshape(blocks * share_rows, model_width), final_gain)
    shared = from_root(normed_final, "section", 0)
    every_row = lax.all_gather(shared, ("tensor", "dp"), axis=0, tiled=True)
    logits = jnp.dot(every_row, unembed, preferred_element_type=jnp.float32)
    vocab_cols = unembed.shape[1]
    target_order = (
        targets.reshape(groups, blocks, tensor_size, share_rows).transpose(2, 0, 1, 3).reshape(-1)
    )
    first_col = lax.axis_index(("section", "tensor", "dp")) * vocab_cols
    matches = target_order[:, None] == first_col + jnp.arange(vocab_cols, dtype=jnp.int32)[None, :]
    picked = jnp.sum(jnp.where(matches, logits, 0.0), axis=-1)
    highest = lax.pmax(jnp.max(logits, axis=-1), ("section", "tensor", "dp"))
    local_total = jnp.sum(jnp.exp(logits - highest[:, None]), axis=-1)
    summed_exp, chosen = lax.psum((local_total, picked), ("section", "tensor", "dp"))
    logprob = chosen - highest - jnp.log(summed_exp)
    return (
        logprob.reshape(tensor_size, groups, blocks, share_rows)
        .transpose(1, 2, 0, 3)
        .reshape(groups, length)
    )


def solution(mesh):
    in_specs = (
        P("dp", None, None),
        P(),
        P(),
        P("section", None),
        P("section", None, ("tensor", "dp")),
        P("section", None, "tensor"),
        P("section", None, "tensor"),
        P("section", ("tensor", "dp"), None),
        P(),
        P(None, ("section", "tensor", "dp")),
    )
    out_specs = P()
    return jax.shard_map(
        on_device, mesh=mesh, in_specs=in_specs, out_specs=out_specs, check_vma=False
    )
```
